32 devices in a mesh: seq: 16 (over z, x, core), fsdp: 2 (over y).
Axes of the slice: x: 2, y: 2, z: 4, core: 2. Of those that a mesh axis runs over, the one named last changes fastest.
Arguments:
- state_in: bfloat16 [2048, 5280], P('seq'), may hold values from -6 to 6
- query_vectors: bfloat16 [2048, 2688], P('seq', 'fsdp'), may hold values from -6 to 6
- key_vectors: bfloat16 [2048, 2688], P('seq', 'fsdp'), may hold values from -6 to 6
- value_weight: bfloat16 [2, 1344, 5280], P('fsdp', 'seq'), may hold values from -0.078125 to 0.078125
- out_weight: bfloat16 [2, 1344, 5280], P('fsdp', 'seq'), may hold values from -0.3125 to 0.3125
- doc_ids: int32 [16], replicated, may hold values from 0 to 4, never falling along the last dimension, each value on 1 to 5 neighbouring positions
- cotangent: bfloat16 [2048, 5280], P('seq'), may hold values from -6 to 6
Outputs:
- final_state: bfloat16 [2048, 5280], P('seq')
- state_grad: float32 [2048, 5280], P('seq')
The draws below stay inside these ranges and needn't reach their ends.
Inputs may be any that keep to these rules, and one draw needn't show every extreme that they name: `doc_ids`: document ids never fall along the blocks; each document covers 1 to 5 consecutive blocks, and some document covers exactly 5.
All inputs are finite; a program needn't handle non-finite values.
Results may differ from the reference program's by a relative error of at most 0.013.
Values may be sent and summed in bfloat16 or wider, within the bound.
A program may use at most 256 MiB of HBM per device.

```python
import math
import jax
import jax.numpy as jnp
import numpy as np
from jax import lax

D = 5280
HEADS = 28
HEAD_DIM = 96
BLOCK = 128
DOC_BLOCKS = 5
UNROLL = 2
TOK_DEV = 128
HEAD_WIDTH = 2688
SEQ_LEN = 2048
NUM_BLOCKS = 16
REACH = 4
DOC_COUNT = 5
N_FSDP = 2


def paired_vectors(key):
    base_seed = jax.random.fold_in(key, 1234)
    seed_query, seed_keys = jax.random.split(base_seed, 2)
    array_shape = (SEQ_LEN, HEAD_WIDTH)
    query_part = jnp.clip(jax.random.normal(seed_query, array_shape, jnp.float32), -6.0, 6.0)
    key_part = jnp.clip(jax.random.normal(seed_keys, array_shape, jnp.float32), -6.0, 6.0)
    return (query_part, key_part)


def draw_query_vectors(key, part):
    return paired_vectors(key)[0].astype(jnp.bfloat16)


def draw_key_vectors(key, part):
    return paired_vectors(key)[1].astype(jnp.bfloat16)


def block_levels(own_key, extent, shards, least, top_value):
    loudness, own = 1.0, jax.random.fold_in(own_key, 6)
    for dim, shards_of in shards:
        draws = jnp.exp(jax.random.uniform(jax.random.fold_in(own, dim), (shards_of,), jnp.float32, least / len(shards), top_value / len(shards)))
        loudness = loudness * jnp.repeat(draws, extent[dim] // shards_of).reshape([-1 if axis == dim else 1 for axis in range(len(extent))])
    return loudness


def profile(amount, total, reach, slope):
    portions = [(1 << 20) // math.isqrt(standing ** slope) + 1 for standing in range(2, amount + 1)]
    rest, given = total - reach - (amount - 1), [1] * (amount - 1)
    while rest > 0:
        candidates = [i for i in range(amount - 1) if given[i] < reach]
        whole, left = sum([portions[i] for i in candidates]), rest
        for i in candidates:
            addition = min(reach - given[i], max(1, left * portions[i] // whole), rest)
            given[i] = given[i] + addition
            rest = rest - addition
    return np.array([reach] + given)


def uneven_parts(rng, amount, total, most, slope):
    if amount == 2:
        one = jax.random.randint(rng, (), max(1, total - most), min(most, total - 1) + 1)
        return jnp.stack([one, total - one])
    tallies = jnp.asarray(profile(amount, total, most, slope), jnp.int32)
    pairs = (amount - 1) // 2
    donor, receiver = tallies[1:1 + 2 * pairs:2], tallies[2:2 + 2 * pairs:2]
    room = jnp.minimum(donor - 1, most - receiver)
    shifted = jax.random.randint(jax.random.fold_in(rng, 1), (pairs,), 0, 1 << 20) % (room + 1)
    tallies = tallies.at[1:1 + 2 * pairs:2].set(donor - shifted).at[2:2 + 2 * pairs:2].set(receiver + shifted)
    return tallies[jax.random.permutation(jax.random.fold_in(rng, 2), amount)]


def bell_draw(stream_key, shape, width, reach, cuts=(), kind=jnp.bfloat16):
    values = jax.random.normal(stream_key, shape, jnp.float32) * width
    if len(cuts) > 0:
        values = block_levels(stream_key, shape, cuts, -0.22, 0.18) * values
    return jnp.clip(values, min=-reach, max=reach).astype(kind)


def setup_inputs(seed: int = 0) -> dict:
    streams_of = jax.random.split(jax.random.key(seed), 8)
    state_in = bell_draw(streams_of[0], (SEQ_LEN, D), 1.0, 6.0, ((0, 16),))
    query_vectors = draw_query_vectors(jax.random.fold_in(streams_of[7], 71), 0)
    key_vectors = draw_key_vectors(jax.random.fold_in(streams_of[7], 71), 0)
    value_weight = bell_draw(streams_of[3], (N_FSDP, HEAD_WIDTH // N_FSDP, D), D ** -0.5, 0.078125, ((0, 2), (1, 16)))
    out_weight = bell_draw(streams_of[4], (N_FSDP, HEAD_WIDTH // N_FSDP, D), (HEAD_WIDTH // 8) ** -0.5, 0.3125, ((0, 2), (1, 16)))
    doc_ids = jnp.searchsorted(jnp.cumsum(uneven_parts(streams_of[5], DOC_COUNT, NUM_BLOCKS, DOC_BLOCKS, 0)), jnp.arange(NUM_BLOCKS), side="right").astype(jnp.int32)
    cotangent = bell_draw(streams_of[6], (SEQ_LEN, D), 1.0, 6.0, ((0, 16),))
    return {"state_in": state_in, "query_vectors": query_vectors, "key_vectors": key_vectors, "value_weight": value_weight, "out_weight": out_weight, "doc_ids": doc_ids, "cotangent": cotangent}


epsilon = 1e-06

def normalize(current):
    mean_square = lax.optimization_barrier(jnp.mean(current * current, axis=-1, keepdims=True))
    inverse_rms = lax.rsqrt(mean_square + epsilon)
    return (current * inverse_rms, inverse_rms)

def rounded(array):
    return lax.optimization_barrier(array.astype(jnp.bfloat16)).astype(jnp.float32)

def grouped(left, right_groups):
    group_width = HEAD_WIDTH // N_FSDP
    running = jnp.zeros((left.shape[0], D), jnp.float32)
    for group in range(N_FSDP):
        columns = left[:, group * group_width:(group + 1) * group_width]
        running = running + rounded(jnp.dot(columns, right_groups[group], preferred_element_type=jnp.float32))
    return running

def reference(state_in, query_vectors, key_vectors, value_weight, out_weight, doc_ids, cotangent):
    rows_here = TOK_DEV
    blocks_here = TOK_DEV // BLOCK
    window_rows = (REACH + 1) * rows_here
    pad_rows = REACH * rows_here
    device_count = SEQ_LEN // TOK_DEV
    value_full = value_weight.reshape(HEAD_WIDTH, D)
    out_full = out_weight.reshape(HEAD_WIDTH, D)
    key_padded = jnp.concatenate([jnp.zeros((pad_rows, HEAD_WIDTH), key_vectors.dtype), key_vectors], 0)
    doc_padded = jnp.concatenate([jnp.full((REACH * blocks_here,), -1, jnp.int32), doc_ids.astype(jnp.int32)])
    query_heads = query_vectors.reshape(device_count, rows_here, HEADS, HEAD_DIM)
    slot_rows = jnp.arange(window_rows)
    query_rows = jnp.arange(rows_here) + pad_rows
    score_scale = 1.0 / math.sqrt(HEAD_DIM)
    device_ids = jnp.arange(device_count, dtype=jnp.int32)

    def device_probs(device):
        start = (device * rows_here).astype(jnp.int32)
        window_keys = lax.dynamic_slice_in_dim(key_padded, start, window_rows, 0).reshape(window_rows, HEADS, HEAD_DIM)
        window_docs = lax.dynamic_slice_in_dim(doc_padded, (device * blocks_here).astype(jnp.int32), (REACH + 1) * blocks_here, 0)
        key_docs = jnp.broadcast_to(window_docs[:, None], ((REACH + 1) * blocks_here, BLOCK)).reshape(-1)
        query_docs = key_docs[pad_rows:]
        allowed = (key_docs[None, :] == query_docs[:, None]) & (slot_rows[None, :] <= query_rows[:, None])
        queries_here = query_heads[device]
        scores = jnp.einsum('qhd,khd->hqk', queries_here.astype(jnp.float32), window_keys.astype(jnp.float32)) * score_scale
        masked = jnp.where(allowed[None], scores, -1e+30)
        maxima = lax.optimization_barrier(jnp.max(masked, axis=2, keepdims=True))
        raised = jnp.where(allowed[None], jnp.exp(masked - maxima), 0.0)
        denominator = lax.optimization_barrier(jnp.sum(raised, axis=2, keepdims=True))
        return (raised / denominator).astype(jnp.bfloat16)
    all_probs = lax.map(device_probs, device_ids)

    def attend(values_b):
        padded = jnp.concatenate([jnp.zeros((pad_rows, HEAD_WIDTH), values_b.dtype), values_b], 0)

        def one_device(device):
            window_values = lax.dynamic_slice_in_dim(padded, (device * rows_here).astype(jnp.int32), window_rows, 0)
            window_values = window_values.reshape(window_rows, HEADS, HEAD_DIM)
            result = jnp.einsum('hqk,khd->qhd', all_probs[device].astype(jnp.float32), window_values.astype(jnp.float32))
            return result.reshape(rows_here, HEAD_WIDTH).astype(jnp.bfloat16)
        return lax.map(one_device, device_ids).reshape(SEQ_LEN, HEAD_WIDTH)

    def spread(d_attended):
        d_heads = d_attended.reshape(device_count, rows_here, HEADS, HEAD_DIM)

        def one_device(device):
            slot_terms = jnp.einsum('hqk,qhd->khd', all_probs[device].astype(jnp.float32), d_heads[device].astype(jnp.float32))
            return slot_terms.reshape(REACH + 1, rows_here, HEAD_WIDTH).astype(jnp.bfloat16)
        all_terms = lax.map(one_device, device_ids)
        running = jnp.zeros((device_count, rows_here, HEAD_WIDTH), jnp.float32)
        for distance in range(REACH + 1):
            contrib = all_terms[distance:, REACH - distance].astype(jnp.float32)
            filler = jnp.zeros((distance, rows_here, HEAD_WIDTH), jnp.float32)
            running = running + jnp.concatenate([contrib, filler], 0)
        return running.reshape(SEQ_LEN, HEAD_WIDTH).astype(jnp.bfloat16)
    value_groups = value_weight
    out_groups = out_weight
    current = state_in.astype(jnp.float32)
    records = []
    for unroll_step in range(UNROLL):
        normed, inverse_rms = normalize(current)
        values_b = lax.dot_general(normed.astype(jnp.bfloat16), value_full, (((1,), (1,)), ((), ())), preferred_element_type=jnp.float32).astype(jnp.bfloat16)
        attended = attend(values_b)
        current = current + grouped(attended, out_groups)
        records.append((normed, inverse_rms))
    final_state = current.astype(jnp.bfloat16)
    gradient = cotangent.astype(jnp.float32)
    for normed, inverse_rms in reversed(records):
        grad_b = gradient.astype(jnp.bfloat16)
        d_attended = lax.dot_general(grad_b, out_full, (((1,), (1,)), ((), ())), preferred_element_type=jnp.float32).astype(jnp.bfloat16)
        dvalues = spread(d_attended)
        d_normed = grouped(dvalues, value_groups)
        gradient = gradient + inverse_rms * (d_normed - normed * lax.optimization_barrier(jnp.mean(d_normed * normed, axis=-1, keepdims=True)))
    return (final_state, gradient)
```

```python
import functools
import math

import jax
import jax.numpy as jnp
from jax import lax
from jax.experimental import pallas as pl
from jax.experimental.pallas import tpu as pltpu
from jax.sharding import PartitionSpec as P

HEAD_DIM = 96
BLOCK = 128
UNROLL = 2
REACH = 4
PLANE = 4
MESH = pl.DeviceIdType.MESH


epsilon = 1e-06


def from_behind(value, axis, steps):
    count = lax.axis_size(axis)
    first, last = (max(0, -steps), min(count, count - steps))
    return lax.ppermute(value, axis, [(source, source + steps) for source in range(first, last)])


def normalize(current):
    mean_square = jnp.mean(current * current, axis=-1, keepdims=True)
    inverse_rms = lax.rsqrt(mean_square + epsilon)
    return (current * inverse_rms, inverse_rms)


def head_total(partial_value):
    own = partial_value.astype(jnp.bfloat16)
    if lax.axis_size("fsdp") != 2:
        return lax.psum(own, "fsdp").astype(jnp.float32)
    other = lax.ppermute(own, "fsdp", [(0, 1), (1, 0)])
    return own.astype(jnp.float32) + other.astype(jnp.float32)


def contract_last(left, right):
    return lax.dot_general(
        left, right, (((1,), (1,)), ((), ())), preferred_element_type=jnp.float32
    )


def gather_kernel(
    lines, wv_ref, wo_ref, full_v, full_o, slots_v, slots_o,
    raw, packed, own_sem, send_z, recv_z, send_x, recv_x, send_c, recv_c, load_sem, store_sem,
):
    me = lax.axis_index("seq")
    group = lax.axis_index("fsdp")
    line, inner = me // PLANE, me % PLANE
    side, core = inner // 2, inner % 2
    rows, width = wv_ref.shape
    shards, slots, fulls = (wv_ref, wo_ref), (slots_v, slots_o), (full_v, full_o)

    def device(other_line, other_side, other_core):
        return (other_line * PLANE + other_side * 2 + other_core, group)

    right, left = device(line + 1, side, core), device(line - 1, side, core)
    across, twin = device(line, 1 - side, core), device(line, side, 1 - core)
    has_right, has_left = line + 1 < lines, line >= 1

    own = [pltpu.make_async_copy(shards[w], slots[w].at[me], own_sem.at[w]) for w in range(2)]
    for copy in own:
        copy.start()
    barrier = pltpu.get_barrier_semaphore()
    for there in (across, twin):
        pl.semaphore_signal(barrier, inc=1, device_id=there, device_id_type=MESH)
    for exists, there in ((has_right, right), (has_left, left)):
        @pl.when(exists)
        def _():
            pl.semaphore_signal(barrier, inc=1, device_id=there, device_id_type=MESH)
    neighbours = 2 + has_right.astype(jnp.int32) + has_left.astype(jnp.int32)
    pl.semaphore_wait(barrier, neighbours)
    for copy in own:
        copy.wait()

    def along(w, origin, way):
        slot = slots[w].at[origin * PLANE + inner]
        return pltpu.make_async_remote_copy(
            src_ref=slot, dst_ref=slot, send_sem=send_z.at[w, way, origin],
            recv_sem=recv_z.at[w, origin], device_id=right if way == 0 else left, device_id_type=MESH)

    def crossing(w, origin, to_me=False):
        slot = slots[w].at[origin * PLANE + ((1 - side) if to_me else side) * 2 + core]
        return pltpu.make_async_remote_copy(
            src_ref=slot, dst_ref=slot, send_sem=send_x.at[w, origin],
            recv_sem=recv_x.at[w, origin], device_id=across, device_id_type=MESH)

    def twinned(w, origin, far, to_me=False):
        which = (1 - side) if far else side
        slot = slots[w].at[origin * PLANE + which * 2 + ((1 - core) if to_me else core)]
        return pltpu.make_async_remote_copy(
            src_ref=slot, dst_ref=slot, send_sem=send_c.at[w, origin, far],
            recv_sem=recv_c.at[w, origin, far], device_id=twin, device_id_type=MESH)

    def arrived(w, origin):
        crossing(w, origin).start()
        twinned(w, origin, 0).start()

    def crossed(w, origin):
        crossing(w, origin, True).wait_recv()
        twinned(w, origin, 1).start()

    def pack(w, origin):
        for far in range(2):
            twinned(w, origin, far, True).wait_recv()
        loads = [
            pltpu.make_async_copy(slots[w].at[origin * PLANE + k], raw.at[k], load_sem.at[k])
            for k in range(PLANE)
        ]
        for copy in loads:
            copy.start()
        for copy in loads:
            copy.wait()
        for low in range(0, width, 384):
            high = min(low + 384, width)
            for k in range(PLANE):
                packed[k * rows:(k + 1) * rows, low:high] = raw[k, :, low:high]
        store = pltpu.make_async_copy(packed, fulls[w].at[origin], store_sem)
        store.start()
        store.wait()

    def forward(w, step):
        for way in range(2):
            origin = line - step if way == 0 else line + step

            @pl.when((origin >= 0) if way == 0 else (origin < lines))
            def _():
                along(w, origin, way).wait_recv()

                @pl.when(has_right if way == 0 else has_left)
                def _():
                    along(w, origin, way).start()
                arrived(w, origin)

    def each(step, act):
        if step == 0:
            act(line)
            return
        for origin, exists in ((line - step, line >= step), (line + step, line + step < lines)):
            pl.when(exists)(functools.partial(act, origin))

    for w in range(2):
        for exists, way in ((has_right, 0), (has_left, 1)):
            @pl.when(exists)
            def _():
                along(w, line, way).start()
        arrived(w, line)
    order = [(step, w) for step in range(lines) for w in range(2)]
    count = len(order)
    for turn in range(2, count + 3):
        if turn < count:
            forward(order[turn][1], order[turn][0])
        if 0 <= turn - 2 < count:
            step, w = order[turn - 2]
            each(step, functools.partial(crossed, w))
        if 0 <= turn - 3 < count:
            step, w = order[turn - 3]
            each(step, functools.partial(pack, w))
    for w in range(2):
        for origin in range(lines):
            crossing(w, origin).wait_send()
            for far in range(2):
                twinned(w, origin, far).wait_send()
        for step in range(lines):
            pl.when(has_right & (line >= step))(lambda: along(w, line - step, 0).wait_send())
            pl.when(has_left & (line + step < lines))(lambda: along(w, line + step, 1).wait_send())


def gather_rows(value_weight, out_weight):
    count = lax.axis_size("seq")
    rows, width = value_weight.shape[1:]
    lines = count // PLANE
    if count % PLANE or (PLANE * rows) % 16 or rows % 2:
        return tuple(
            lax.all_gather(weight, "seq", axis=1, tiled=True)[0]
            for weight in (value_weight, out_weight)
        )
    full = jax.ShapeDtypeStruct((lines, PLANE * rows, width), jnp.bfloat16)
    slot = jax.ShapeDtypeStruct((count, rows, width), jnp.bfloat16)
    dma = pltpu.SemaphoreType.DMA
    full_v, full_o, _, _ = pl.pallas_call(
        functools.partial(gather_kernel, lines),
        out_shape=(full, full, slot, slot),
        in_specs=[pl.BlockSpec(memory_space=pl.ANY)] * 2,
        out_specs=[pl.BlockSpec(memory_space=pl.ANY)] * 4,
        scratch_shapes=[
            pltpu.VMEM((PLANE, rows, width), jnp.bfloat16),
            pltpu.VMEM((PLANE * rows, width), jnp.bfloat16),
            dma((2,)),
            dma((2, 2, lines)), dma((2, lines)),
            dma((2, lines)), dma((2, lines)),
            dma((2, lines, 2)), dma((2, lines, 2)),
            dma((PLANE,)), dma,
        ],
        compiler_params=pltpu.CompilerParams(
            collective_id=0, has_side_effects=True, vmem_limit_bytes=40 * 1024 * 1024
        ),
    )(value_weight[0], out_weight[0])
    return full_v.reshape(count * rows, width), full_o.reshape(count * rows, width)


def fetch_first(pair):
    return [from_behind((pair[0], pair[1]), "seq", distance) for distance in range(REACH, 0, -1)]


def fetch_later(values_b):
    return [from_behind(values_b, "seq", distance) for distance in range(REACH, 0, -1)]


def local(state_in, query_vectors, key_vectors, value_weight, out_weight, doc_ids, cotangent):
    rows_here = state_in.shape[0]
    blocks_here = rows_here // BLOCK
    width_here = query_vectors.shape[1]
    heads_here = width_here // HEAD_DIM
    window_rows = (REACH + 1) * rows_here
    pad_rows = REACH * rows_here
    device_index = lax.axis_index("seq")
    score_scale = 1.0 / math.sqrt(HEAD_DIM)
    doc_padded = jnp.concatenate([jnp.full((REACH * blocks_here,), -1, jnp.int32), doc_ids])
    window_docs = lax.dynamic_slice_in_dim(
        doc_padded, device_index * blocks_here, (REACH + 1) * blocks_here, 0
    )
    key_docs = jnp.broadcast_to(window_docs[:, None], ((REACH + 1) * blocks_here, BLOCK)).reshape(
        -1
    )
    query_docs = key_docs[pad_rows:]
    slot_rows = jnp.arange(window_rows)
    query_rows = jnp.arange(rows_here) + pad_rows
    allowed = (key_docs[None, :] == query_docs[:, None]) & (
        slot_rows[None, :] <= query_rows[:, None]
    )
    value_rows, out_rows = gather_rows(value_weight, out_weight)
    current = state_in.astype(jnp.float32)
    records = []
    soft_weights = None
    for unroll_step in range(UNROLL):
        normed, inverse_rms = normalize(current)
        values_b = contract_last(normed.astype(jnp.bfloat16), value_rows).astype(jnp.bfloat16)
        if unroll_step == 0:
            received = fetch_first((key_vectors, values_b))
            window_keys = jnp.concatenate([pair[0] for pair in received] + [key_vectors], 0)
            window_values = jnp.concatenate([pair[1] for pair in received] + [values_b], 0)
            query_heads = query_vectors.reshape(rows_here, heads_here, HEAD_DIM)
            key_heads = window_keys.reshape(window_rows, heads_here, HEAD_DIM)
            scores = (
                jnp.einsum(
                    "qhd,khd->hqk", query_heads, key_heads, preferred_element_type=jnp.float32
                )
                * score_scale
            )
            masked = jnp.where(allowed[None], scores, -1e30)
            maxima = jnp.max(masked, axis=2, keepdims=True)
            raised = jnp.where(allowed[None], jnp.exp(masked - maxima), 0.0)
            denominator = jnp.sum(raised, axis=2, keepdims=True)
            soft_weights = (raised / denominator).astype(jnp.bfloat16)
        else:
            received = fetch_later(values_b)
            window_values = jnp.concatenate(received + [values_b], 0)
        attended = jnp.einsum(
            "hqk,khd->qhd",
            soft_weights,
            window_values.reshape(window_rows, heads_here, HEAD_DIM),
            preferred_element_type=jnp.float32,
        )
        attended = attended.reshape(rows_here, width_here).astype(jnp.bfloat16)
        current = current + head_total(
            jnp.dot(attended, out_rows, preferred_element_type=jnp.float32)
        )
        records.append((normed, inverse_rms))
    final_state = current.astype(jnp.bfloat16)
    gradient = cotangent.astype(jnp.float32)
    for normed, inverse_rms in reversed(records):
        grad_b = gradient.astype(jnp.bfloat16)
        d_attended = contract_last(grad_b, out_rows).astype(jnp.bfloat16)
        slot_terms = jnp.einsum(
            "hqk,qhd->khd",
            soft_weights,
            d_attended.reshape(rows_here, heads_here, HEAD_DIM),
            preferred_element_type=jnp.float32,
        )
        slot_terms = slot_terms.reshape(REACH + 1, rows_here, width_here).astype(jnp.bfloat16)
        returned = [
            from_behind(slot_terms[REACH - distance], "seq", -distance)
            for distance in range(1, REACH + 1)
        ]
        running = slot_terms[REACH].astype(jnp.float32)
        for piece_back in returned:
            running = running + piece_back.astype(jnp.float32)
        dvalues = running.astype(jnp.bfloat16)
        d_normed = head_total(jnp.dot(dvalues, value_rows, preferred_element_type=jnp.float32))
        gradient = gradient + inverse_rms * (
            d_normed - normed * jnp.mean(d_normed * normed, axis=-1, keepdims=True)
        )
    return (final_state, gradient)


def solution(mesh):
    placed = (
        P("seq", None),
        P("seq", "fsdp"),
        P("seq", "fsdp"),
        P("fsdp", "seq", None),
        P("fsdp", "seq", None),
        P(),
        P("seq", None),
    )
    return jax.shard_map(
        local,
        mesh=mesh,
        in_specs=placed,
        out_specs=(P("seq", None), P("seq", None)),
        check_vma=False,
    )
```

```python
import functools
import math

import jax
import jax.numpy as jnp
from jax import lax
from jax.experimental import pallas as pl
from jax.experimental.pallas import tpu as pltpu
from jax.sharding import PartitionSpec as P

HEAD_DIM = 96
BLOCK = 128
UNROLL = 2
REACH = 4
PLANE = 4
MESH = pl.DeviceIdType.MESH


epsilon = 1e-06


def from_behind(value, axis, steps):
    count = lax.axis_size(axis)
    first, last = (max(0, -steps), min(count, count - steps))
    return lax.ppermute(value, axis, [(source, source + steps) for source in range(first, last)])


def normalize(current):
    mean_square = jnp.mean(current * current, axis=0, keepdims=True)
    inverse_rms = lax.rsqrt(mean_square + epsilon)
    return (current * inverse_rms, inverse_rms)


def head_total(partial_value):
    own = partial_value.astype(jnp.bfloat16)
    if lax.axis_size("fsdp") != 2:
        return lax.psum(own, "fsdp").astype(jnp.float32)
    other = lax.ppermute(own, "fsdp", [(0, 1), (1, 0)])
    return own.astype(jnp.float32) + other.astype(jnp.float32)


def from_twin(value):
    count = lax.axis_size("seq")
    return lax.ppermute(value, "seq", [(source, source ^ 1) for source in range(count)])


def window_of(value, odd):
    first, second = from_behind(value, "seq", 2), from_behind(value, "seq", 4)
    low = from_twin(jnp.where(odd, second, first))
    high = from_twin(jnp.where(odd, first, value))
    return jnp.concatenate([second, low, first, high, value], 1)


def returned_sum(terms, odd):
    low, high = from_twin(terms[1]), from_twin(terms[3])
    wide = [term.astype(jnp.float32) for term in (terms[0], terms[2], terms[4], low, high)]
    farther = wide[0] + jnp.where(odd, wide[3], 0.0)
    nearer = wide[1] + jnp.where(odd, wide[4], wide[3])
    here = wide[2] + jnp.where(odd, 0.0, wide[4])
    nearer = from_behind(nearer.astype(jnp.bfloat16), "seq", -2)
    farther = from_behind(farther.astype(jnp.bfloat16), "seq", -4)
    return here + nearer.astype(jnp.float32) + farther.astype(jnp.float32)


def times(weights, columns):
    return jnp.dot(weights, columns, preferred_element_type=jnp.float32)


def times_across(weights, columns):
    return lax.dot_general(
        weights, columns, (((0,), (0,)), ((), ())), preferred_element_type=jnp.float32
    )


def gather_kernel(
    lines, wv_ref, wo_ref, state_ref, grad_ref, keys_ref,
    full_v, full_o, slots_v, slots_o, product_v, product_o, window, raw, packed, own_sem, send_z, recv_z, send_x, recv_x, send_c, recv_c, load_sem, store_sem,
    key_send, key_recv, key_own,
):
    me = lax.axis_index("seq")
    group = lax.axis_index("fsdp")
    line, inner = me // PLANE, me % PLANE
    side, core = inner // 2, inner % 2
    rows, width = wv_ref.shape
    shards, slots, fulls = (wv_ref, wo_ref), (slots_v, slots_o), (full_v, full_o)

    def device(other_line, other_side, other_core):
        return (other_line * PLANE + other_side * 2 + other_core, group)

    right, left = device(line + 1, side, core), device(line - 1, side, core)
    across, twin = device(line, 1 - side, core), device(line, side, 1 - core)
    has_right, has_left = line + 1 < lines, line >= 1

    diagonal = device(line + 2 * side - 1, 1 - side, core)
    has_diagonal = ((side == 1) & has_right) | ((side == 0) & has_left)
    factors, products = (state_ref, grad_ref), (product_v, product_o)
    span = keys_ref.shape[1]

    own = [pltpu.make_async_copy(shards[w], slots[w].at[me], own_sem.at[w]) for w in range(2)]
    for copy in own:
        copy.start()
    barrier = pltpu.get_barrier_semaphore()
    for there in (across, twin):
        pl.semaphore_signal(barrier, inc=1, device_id=there, device_id_type=MESH)
    for exists, there in ((has_right, right), (has_left, left), (has_diagonal, diagonal)):
        @pl.when(exists)
        def _():
            pl.semaphore_signal(barrier, inc=1, device_id=there, device_id_type=MESH)
    neighbours = 2 + sum(there.astype(jnp.int32) for there in (has_right, has_left, has_diagonal))
    pl.semaphore_wait(barrier, neighbours)
    for copy in own:
        copy.wait()

    def place(number):
        return window.at[:, number * span:(number + 1) * span]

    def key_copy(source, number, there):
        return pltpu.make_async_remote_copy(
            src_ref=source, dst_ref=place(number), send_sem=key_send.at[number],
            recv_sem=key_recv.at[number], device_id=there, device_id_type=MESH)

    count = lines * PLANE
    second = (line * PLANE + inner + 2) // PLANE
    ahead = (second * PLANE + (1 - side) * 2 + core, group)
    key_here = pltpu.make_async_copy(keys_ref, place(REACH), key_own)
    odd = core == 1

    def twin_keys(act):
        pl.when(odd & (me >= 4))(lambda: act(key_copy(place(0), 1, twin)))
        pl.when(odd & (me >= 2))(lambda: act(key_copy(place(2), 3, twin)))
        pl.when((core == 0) & (me >= 2))(lambda: act(key_copy(place(2), 1, twin)))
        pl.when(core == 0)(lambda: act(key_copy(keys_ref, 3, twin)))

    def along(w, origin, way):
        slot = slots[w].at[origin * PLANE + inner]
        return pltpu.make_async_remote_copy(
            src_ref=slot, dst_ref=slot, send_sem=send_z.at[w, way, origin],
            recv_sem=recv_z.at[w, origin], device_id=right if way == 0 else left, device_id_type=MESH)

    def crossing(w, origin, to_me=False):
        slot = slots[w].at[origin * PLANE + ((1 - side) if to_me else side) * 2 + core]
        return pltpu.make_async_remote_copy(
            src_ref=slot, dst_ref=slot, send_sem=send_x.at[w, origin],
            recv_sem=recv_x.at[w, origin], device_id=across, device_id_type=MESH)

    def twinned(w, origin, far, to_me=False):
        which = (1 - side) if far else side
        slot = slots[w].at[origin * PLANE + which * 2 + ((1 - core) if to_me else core)]
        return pltpu.make_async_remote_copy(
            src_ref=slot, dst_ref=slot, send_sem=send_c.at[w, origin, far],
            recv_sem=recv_c.at[w, origin, far], device_id=twin, device_id_type=MESH)

    def arrived(w, origin):
        crossing(w, origin).start()
        twinned(w, origin, 0).start()

    def crossed(w, origin):
        crossing(w, origin, True).wait_recv()
        twinned(w, origin, 1).start()

    def pack(w, origin):
        for far in range(2):
            twinned(w, origin, far, True).wait_recv()
        loads = [
            pltpu.make_async_copy(slots[w].at[origin * PLANE + k], raw.at[k], load_sem.at[k])
            for k in range(PLANE)
        ]
        for copy in loads:
            copy.start()
        for copy in loads:
            copy.wait()
        for low in range(0, width, 384):
            high = min(low + 384, width)
            for k in range(PLANE):
                packed[k * rows:(k + 1) * rows, low:high] = raw[k, :, low:high]
        store = pltpu.make_async_copy(packed, fulls[w].at[origin], store_sem)
        store.start()
        products[w][origin] = jnp.dot(
            packed[...], factors[w][...], preferred_element_type=jnp.float32
        )
        store.wait()

    def forward(w, step):
        for way in range(2):
            origin = line - step if way == 0 else line + step

            @pl.when((origin >= 0) if way == 0 else (origin < lines))
            def _():
                along(w, origin, way).wait_recv()

                @pl.when(has_right if way == 0 else has_left)
                def _():
                    along(w, origin, way).start()
                arrived(w, origin)

    def each(step, act):
        if step == 0:
            act(line)
            return
        for origin, exists in ((line - step, line >= step), (line + step, line + step < lines)):
            pl.when(exists)(functools.partial(act, origin))

    for w in range(2):
        for exists, way in ((has_right, 0), (has_left, 1)):
            @pl.when(exists)
            def _():
                along(w, line, way).start()
        arrived(w, line)
    key_here.start()
    pl.when(me + 2 < count)(lambda: key_copy(keys_ref, 2, ahead).start())
    pl.when(has_right)(lambda: key_copy(keys_ref, 0, right).start())
    order = [(step, w) for step in range(lines) for w in range(2)]
    turns = len(order)
    for turn in range(2, turns + 3):
        if turn < turns:
            forward(order[turn][1], order[turn][0])
        if 0 <= turn - 2 < turns:
            step, w = order[turn - 2]
            each(step, functools.partial(crossed, w))
        if 0 <= turn - 3 < turns:
            step, w = order[turn - 3]
            each(step, functools.partial(pack, w))
        if turn == 5:
            pl.when(me >= 2)(lambda: key_copy(keys_ref, 2, ahead).wait_recv())
            pl.when(me >= 4)(lambda: key_copy(keys_ref, 0, right).wait_recv())
            twin_keys(lambda copy: copy.start())
    pl.when(me >= 3)(lambda: key_copy(keys_ref, 1, twin).wait_recv())
    pl.when(me >= 1)(lambda: key_copy(keys_ref, 3, twin).wait_recv())
    twin_keys(lambda copy: copy.wait_send())
    pl.when(me + 2 < count)(lambda: key_copy(keys_ref, 2, ahead).wait_send())
    pl.when(has_right)(lambda: key_copy(keys_ref, 0, right).wait_send())
    key_here.wait()
    for w in range(2):
        for origin in range(lines):
            crossing(w, origin).wait_send()
            for far in range(2):
                twinned(w, origin, far).wait_send()
        for step in range(lines):
            pl.when(has_right & (line >= step))(lambda: along(w, line - step, 0).wait_send())
            pl.when(has_left & (line + step < lines))(lambda: along(w, line + step, 1).wait_send())


def gather_rows(value_weight, out_weight, state, gradient, keys, odd):
    count = lax.axis_size("seq")
    rows, width = value_weight.shape[1:]
    tokens, channels = state.shape[1], keys.shape[0]
    lines = count // PLANE
    if count % PLANE or (PLANE * rows) % 16 or rows % 2:
        value_rows, out_rows = (
            lax.all_gather(weight, "seq", axis=1, tiled=True)[0]
            for weight in (value_weight, out_weight)
        )
        window = window_of(keys, odd)
        return value_rows, out_rows, times(value_rows, state), times(out_rows, gradient), window
    full = jax.ShapeDtypeStruct((lines, PLANE * rows, width), jnp.bfloat16)
    slot = jax.ShapeDtypeStruct((count, rows, width), jnp.bfloat16)
    product = jax.ShapeDtypeStruct((lines, PLANE * rows, tokens), jnp.float32)
    window = jax.ShapeDtypeStruct((channels, (REACH + 1) * tokens), jnp.bfloat16)
    dma = pltpu.SemaphoreType.DMA
    anywhere, vector = (pl.BlockSpec(memory_space=space) for space in (pl.ANY, pltpu.VMEM))
    full_v, full_o, _, _, values, d_attended, window = pl.pallas_call(
        functools.partial(gather_kernel, lines),
        out_shape=(full, full, slot, slot, product, product, window),
        in_specs=[anywhere, anywhere, vector, vector, anywhere],
        out_specs=[anywhere] * 4 + [vector, vector, anywhere],
        scratch_shapes=[
            pltpu.VMEM((PLANE, rows, width), jnp.bfloat16),
            pltpu.VMEM((PLANE * rows, width), jnp.bfloat16),
            dma((2,)),
            dma((2, 2, lines)), dma((2, lines)),
            dma((2, lines)), dma((2, lines)),
            dma((2, lines, 2)), dma((2, lines, 2)),
            dma((PLANE,)), dma,
            dma((REACH,)), dma((REACH,)), dma,
        ],
        compiler_params=pltpu.CompilerParams(
            collective_id=0, has_side_effects=True, vmem_limit_bytes=48 * 1024 * 1024
        ),
    )(value_weight[0], out_weight[0], state, gradient, keys)
    return (
        full_v.reshape(count * rows, width),
        full_o.reshape(count * rows, width),
        values.reshape(count * rows, tokens),
        d_attended.reshape(count * rows, tokens),
        window,
    )


def local(state_in, query_vectors, key_vectors, value_weight, out_weight, doc_ids, cotangent):
    rows_here = state_in.shape[0]
    blocks_here = rows_here // BLOCK
    width_here = query_vectors.shape[1]
    heads_here = width_here // HEAD_DIM
    window_rows = (REACH + 1) * rows_here
    pad_rows = REACH * rows_here
    device_index = lax.axis_index("seq")
    odd = device_index % 2 == 1
    score_scale = 1.0 / math.sqrt(HEAD_DIM)
    doc_padded = jnp.concatenate([jnp.full((REACH * blocks_here,), -1, jnp.int32), doc_ids])
    window_docs = lax.dynamic_slice_in_dim(
        doc_padded, device_index * blocks_here, (REACH + 1) * blocks_here, 0
    )
    key_docs = jnp.broadcast_to(window_docs[:, None], ((REACH + 1) * blocks_here, BLOCK)).reshape(
        -1
    )
    query_docs = key_docs[pad_rows:]
    slot_rows = jnp.arange(window_rows)
    query_rows = jnp.arange(rows_here) + pad_rows
    allowed = (key_docs[None, :] == query_docs[:, None]) & (
        slot_rows[None, :] <= query_rows[:, None]
    )
    value_rows, out_rows, raw_values, raw_gradient, window_keys = gather_rows(
        value_weight, out_weight, state_in.T, cotangent.T, key_vectors.T, odd
    )
    current = state_in.T.astype(jnp.float32)
    normed, inverse_rms = normalize(current)
    values = (raw_values * inverse_rms).astype(jnp.bfloat16)
    window_values = window_of(values, odd)
    query_heads = query_vectors.T.reshape(heads_here, HEAD_DIM, rows_here)
    key_heads = window_keys.reshape(heads_here, HEAD_DIM, window_rows)
    scores = (
        jnp.einsum("hdq,hdk->hqk", query_heads, key_heads, preferred_element_type=jnp.float32)
        * score_scale
    )
    masked = jnp.where(allowed[None], scores, -1e30)
    maxima = jnp.max(masked, axis=2, keepdims=True)
    raised = jnp.where(allowed[None], jnp.exp(masked - maxima), 0.0)
    denominator = jnp.sum(raised, axis=2, keepdims=True)
    soft_weights = (raised / denominator).astype(jnp.bfloat16)

    def attend(window_values):
        attended = jnp.einsum(
            "hqk,hdk->hdq",
            soft_weights,
            window_values.reshape(heads_here, HEAD_DIM, window_rows),
            preferred_element_type=jnp.float32,
        )
        return attended.reshape(width_here, rows_here).astype(jnp.bfloat16)

    def spread(d_attended):
        heads = d_attended.astype(jnp.bfloat16).reshape(heads_here, HEAD_DIM, rows_here)
        terms = jnp.einsum("hqk,hdq->hdk", soft_weights, heads, preferred_element_type=jnp.float32)
        terms = terms.reshape(width_here, window_rows).astype(jnp.bfloat16)
        return [
            terms[:, slot * rows_here:(slot + 1) * rows_here] for slot in range(REACH + 1)
        ]

    gradient = cotangent.T.astype(jnp.float32)
    records = []
    for unroll_step in range(UNROLL):
        terms = spread(raw_gradient)
        records.append((normed, inverse_rms))
        update = times_across(out_rows, attend(window_values))
        dvalues = returned_sum(terms, odd).astype(jnp.bfloat16)
        dvalues, update = lax.optimization_barrier((dvalues, update.astype(jnp.bfloat16)))
        partial_grad = times_across(value_rows, dvalues)
        current = current + head_total(update)
        d_normed = head_total(partial_grad)
        normed, inverse_rms = (None, None)
        if unroll_step + 1 < UNROLL:
            normed, inverse_rms = normalize(current)
        turn = UNROLL - 1 - unroll_step
        normed_turn, inverse_turn = (
            records[turn] if turn < len(records) else (normed, inverse_rms)
        )
        gradient = gradient + inverse_turn * (
            d_normed - normed_turn * jnp.mean(d_normed * normed_turn, axis=0, keepdims=True)
        )
        if unroll_step + 1 < UNROLL:
            window_values = window_of(
                times(value_rows, normed.astype(jnp.bfloat16)).astype(jnp.bfloat16), odd
            )
            raw_gradient = times(out_rows, gradient.astype(jnp.bfloat16))
    return (current.astype(jnp.bfloat16).T, gradient.T)


def solution(mesh):
    placed = (
        P("seq", None),
        P("seq", "fsdp"),
        P("seq", "fsdp"),
        P("fsdp", "seq", None),
        P("fsdp", "seq", None),
        P(),
        P("seq", None),
    )
    return jax.shard_map(
        local,
        mesh=mesh,
        in_specs=placed,
        out_specs=(P("seq", None), P("seq", None)),
        check_vma=False,
    )
```

```python
import functools
import math

import jax
import jax.numpy as jnp
from jax import lax
from jax.experimental import pallas as pl
from jax.experimental.pallas import tpu as pltpu
from jax.sharding import PartitionSpec as P

HEAD_DIM = 96
BLOCK = 128
UNROLL = 2
REACH = 4
PLANE = 4
MESH = pl.DeviceIdType.MESH


epsilon = 1e-06


def from_behind(value, axis, steps):
    count = lax.axis_size(axis)
    first, last = (max(0, -steps), min(count, count - steps))
    return lax.ppermute(value, axis, [(source, source + steps) for source in range(first, last)])


def normalize(current):
    mean_square = jnp.mean(current * current, axis=0, keepdims=True)
    inverse_rms = lax.rsqrt(mean_square + epsilon)
    return (current * inverse_rms, inverse_rms)


def other_group(own):
    if lax.axis_size("fsdp") != 2:
        wide = own.astype(jnp.float32)
        return lax.psum(wide, "fsdp") - wide
    return lax.ppermute(own, "fsdp", [(0, 1), (1, 0)])


def head_total(own, other):
    return own.astype(jnp.float32) + other.astype(jnp.float32)


def from_twin(value):
    count = lax.axis_size("seq")
    return lax.ppermute(value, "seq", [(source, source ^ 1) for source in range(count)])


def window_of(value, odd):
    first, second = from_behind(value, "seq", 2), from_behind(value, "seq", 4)
    low = from_twin(jnp.where(odd, second, first))
    high = from_twin(jnp.where(odd, first, value))
    return jnp.concatenate([second, low, first, high, value], 1)


def returned_sum(terms, update, odd):
    low, high = from_twin(terms[1]), from_twin(terms[3])
    low, high, update = lax.optimization_barrier((low, high, update))
    wide = [term.astype(jnp.float32) for term in (terms[0], terms[2], terms[4], low, high)]
    farther = wide[0] + jnp.where(odd, wide[3], 0.0)
    nearer = wide[1] + jnp.where(odd, wide[4], wide[3])
    here = wide[2] + jnp.where(odd, 0.0, wide[4])
    nearer = from_behind(nearer.astype(jnp.bfloat16), "seq", -2)
    farther = from_behind(farther.astype(jnp.bfloat16), "seq", -4)
    total = here + nearer.astype(jnp.float32) + farther.astype(jnp.float32)
    return total.astype(jnp.bfloat16), update


def times(weights, columns):
    return jnp.dot(weights, columns, preferred_element_type=jnp.float32)


def times_across(weights, columns):
    return lax.dot_general(
        weights, columns, (((0,), (0,)), ((), ())), preferred_element_type=jnp.float32
    )


def gather_kernel(
    lines, wv_ref, wo_ref, state_ref, grad_ref, keys_ref,
    full_v, full_o, slots_v, slots_o, product_v, product_o, window, raw, packed, own_sem, send_z, recv_z, send_x, recv_x, send_c, recv_c, load_sem, store_sem,
    key_send, key_recv, key_own, send_y, recv_y,
):
    me = lax.axis_index("seq")
    group = lax.axis_index("fsdp")
    line, inner = me // PLANE, me % PLANE
    side, core = inner // 2, inner % 2
    rows, width = wv_ref.shape
    early = width // 6 // 128 * 128
    shards, slots, fulls = (wv_ref, wo_ref), (slots_v, slots_o), (full_v, full_o)

    def device(other_line, other_side, other_core):
        return (other_line * PLANE + other_side * 2 + other_core, group)

    right, left = device(line + 1, side, core), device(line - 1, side, core)
    across, twin = device(line, 1 - side, core), device(line, side, 1 - core)
    has_right, has_left = line + 1 < lines, line >= 1

    diagonal = device(line + 2 * side - 1, 1 - side, core)
    has_diagonal = ((side == 1) & has_right) | ((side == 0) & has_left)
    factors, products = (state_ref, grad_ref), (product_v, product_o)
    span = keys_ref.shape[1]

    own = [pltpu.make_async_copy(shards[w], slots[w].at[me], own_sem.at[w]) for w in range(2)]
    for copy in own:
        copy.start()
    barrier = pltpu.get_barrier_semaphore()
    for there in (across, twin):
        pl.semaphore_signal(barrier, inc=1, device_id=there, device_id_type=MESH)
    for exists, there in ((has_right, right), (has_left, left), (has_diagonal, diagonal)):
        @pl.when(exists)
        def _():
            pl.semaphore_signal(barrier, inc=1, device_id=there, device_id_type=MESH)
    neighbours = 2 + sum(there.astype(jnp.int32) for there in (has_right, has_left, has_diagonal))
    pl.semaphore_wait(barrier, neighbours)
    for copy in own:
        copy.wait()

    def place(number):
        return window.at[:, number * span:(number + 1) * span]

    def key_copy(source, number, there):
        return pltpu.make_async_remote_copy(
            src_ref=source, dst_ref=place(number), send_sem=key_send.at[number],
            recv_sem=key_recv.at[number], device_id=there, device_id_type=MESH)

    count = lines * PLANE
    second = (line * PLANE + inner + 2) // PLANE
    ahead = (second * PLANE + (1 - side) * 2 + core, group)
    key_here = pltpu.make_async_copy(keys_ref, place(REACH), key_own)
    odd = core == 1

    def twin_keys(act):
        pl.when(odd & (me >= 4))(lambda: act(key_copy(place(0), 1, twin)))
        pl.when(odd & (me >= 2))(lambda: act(key_copy(place(2), 3, twin)))
        pl.when((core == 0) & (me >= 2))(lambda: act(key_copy(place(2), 1, twin)))
        pl.when(core == 0)(lambda: act(key_copy(keys_ref, 3, twin)))

    def along(w, origin, way):
        slot = slots[w].at[origin * PLANE + inner]
        return pltpu.make_async_remote_copy(
            src_ref=slot, dst_ref=slot, send_sem=send_z.at[w, way, origin],
            recv_sem=recv_z.at[w, origin], device_id=right if way == 0 else left, device_id_type=MESH)

    def along_side(w, origin, way):
        slot = slots[w].at[origin * PLANE + (1 - side) * 2 + core, :, :early]
        return pltpu.make_async_remote_copy(
            src_ref=slot, dst_ref=slot, send_sem=send_y.at[w, way, origin],
            recv_sem=recv_y.at[w, origin], device_id=right if way == 0 else left, device_id_type=MESH)

    def crossing(w, origin, whole, to_me=False):
        index = origin * PLANE + ((1 - side) if to_me else side) * 2 + core
        slot = slots[w].at[index] if whole else slots[w].at[index, :, early:]
        return pltpu.make_async_remote_copy(
            src_ref=slot, dst_ref=slot, send_sem=send_x.at[w, origin],
            recv_sem=recv_x.at[w, origin], device_id=across, device_id_type=MESH)

    def twinned(w, origin, far, to_me=False):
        which = (1 - side) if far else side
        slot = slots[w].at[origin * PLANE + which * 2 + ((1 - core) if to_me else core)]
        return pltpu.make_async_remote_copy(
            src_ref=slot, dst_ref=slot, send_sem=send_c.at[w, origin, far],
            recv_sem=recv_c.at[w, origin, far], device_id=twin, device_id_type=MESH)

    def arrived(w, origin, whole):
        crossing(w, origin, whole).start()
        twinned(w, origin, 0).start()

    def crossed(w, origin, way):
        crossing(w, origin, way is None, True).wait_recv()
        if way is not None:
            along_side(w, origin, way).wait_recv()
        if way != 1:
            pl.when(has_right)(lambda: along_side(w, origin, 0).start())
        if way != 0:
            pl.when(has_left)(lambda: along_side(w, origin, 1).start())
        twinned(w, origin, 1).start()

    def pack(w, origin, way):
        for far in range(2):
            twinned(w, origin, far, True).wait_recv()
        loads = [
            pltpu.make_async_copy(slots[w].at[origin * PLANE + k], raw.at[k], load_sem.at[k])
            for k in range(PLANE)
        ]
        for copy in loads:
            copy.start()
        for copy in loads:
            copy.wait()
        for low in range(0, width, 384):
            high = min(low + 384, width)
            for k in range(PLANE):
                packed[k * rows:(k + 1) * rows, low:high] = raw[k, :, low:high]
        store = pltpu.make_async_copy(packed, fulls[w].at[origin], store_sem)
        store.start()
        products[w][origin] = jnp.dot(
            packed[...], factors[w][...], preferred_element_type=jnp.float32
        )
        store.wait()

    def forward(w, step):
        for way in range(2):
            origin = line - step if way == 0 else line + step

            @pl.when((origin >= 0) if way == 0 else (origin < lines))
            def _():
                along(w, origin, way).wait_recv()

                @pl.when(has_right if way == 0 else has_left)
                def _():
                    along(w, origin, way).start()
                arrived(w, origin, False)

    def each(step, act):
        if step == 0:
            act(line, None)
            return
        pl.when(line >= step)(lambda: act(line - step, 0))
        pl.when(line + step < lines)(lambda: act(line + step, 1))

    for w in range(2):
        for exists, way in ((has_right, 0), (has_left, 1)):
            @pl.when(exists)
            def _():
                along(w, line, way).start()
        arrived(w, line, True)
    key_here.start()
    pl.when(me + 2 < count)(lambda: key_copy(keys_ref, 2, ahead).start())
    pl.when(has_right)(lambda: key_copy(keys_ref, 0, right).start())
    order = [(step, w) for step in range(lines) for w in range(2)]
    turns = len(order)
    for turn in range(2, turns + 3):
        if turn < turns:
            forward(order[turn][1], order[turn][0])
        if 0 <= turn - 2 < turns:
            step, w = order[turn - 2]
            each(step, functools.partial(crossed, w))
        if 0 <= turn - 3 < turns:
            step, w = order[turn - 3]
            each(step, functools.partial(pack, w))
        if turn == 5:
            pl.when(me >= 2)(lambda: key_copy(keys_ref, 2, ahead).wait_recv())
            pl.when(me >= 4)(lambda: key_copy(keys_ref, 0, right).wait_recv())
            twin_keys(lambda copy: copy.start())
    pl.when(me >= 3)(lambda: key_copy(keys_ref, 1, twin).wait_recv())
    pl.when(me >= 1)(lambda: key_copy(keys_ref, 3, twin).wait_recv())
    twin_keys(lambda copy: copy.wait_send())
    pl.when(me + 2 < count)(lambda: key_copy(keys_ref, 2, ahead).wait_send())
    pl.when(has_right)(lambda: key_copy(keys_ref, 0, right).wait_send())
    key_here.wait()
    for w in range(2):
        for origin in range(lines):
            for whole in (True, False):
                pl.when((line == origin) if whole else (line != origin))(
                    functools.partial(crossing(w, origin, whole).wait_send)
                )
            for far in range(2):
                twinned(w, origin, far).wait_send()
        for step in range(lines):
            for move in (along, along_side):
                pl.when(has_right & (line >= step))(lambda: move(w, line - step, 0).wait_send())
                pl.when(has_left & (line + step < lines))(
                    lambda: move(w, line + step, 1).wait_send()
                )


def gather_rows(value_weight, out_weight, state, gradient, keys, odd):
    count = lax.axis_size("seq")
    rows, width = value_weight.shape[1:]
    tokens, channels = state.shape[1], keys.shape[0]
    lines = count // PLANE
    if count % PLANE or (PLANE * rows) % 16 or rows % 2:
        value_rows, out_rows = (
            lax.all_gather(weight, "seq", axis=1, tiled=True)[0]
            for weight in (value_weight, out_weight)
        )
        window = window_of(keys, odd)
        return value_rows, out_rows, times(value_rows, state), times(out_rows, gradient), window
    full = jax.ShapeDtypeStruct((lines, PLANE * rows, width), jnp.bfloat16)
    slot = jax.ShapeDtypeStruct((count, rows, width), jnp.bfloat16)
    product = jax.ShapeDtypeStruct((lines, PLANE * rows, tokens), jnp.float32)
    window = jax.ShapeDtypeStruct((channels, (REACH + 1) * tokens), jnp.bfloat16)
    dma = pltpu.SemaphoreType.DMA
    anywhere, vector = (pl.BlockSpec(memory_space=space) for space in (pl.ANY, pltpu.VMEM))
    full_v, full_o, _, _, values, d_attended, window = pl.pallas_call(
        functools.partial(gather_kernel, lines),
        out_shape=(full, full, slot, slot, product, product, window),
        in_specs=[anywhere, anywhere, vector, vector, anywhere],
        out_specs=[anywhere] * 4 + [vector, vector, anywhere],
        scratch_shapes=[
            pltpu.VMEM((PLANE, rows, width), jnp.bfloat16),
            pltpu.VMEM((PLANE * rows, width), jnp.bfloat16),
            dma((2,)),
            dma((2, 2, lines)), dma((2, lines)),
            dma((2, lines)), dma((2, lines)),
            dma((2, lines, 2)), dma((2, lines, 2)),
            dma((PLANE,)), dma,
            dma((REACH,)), dma((REACH,)), dma,
            dma((2, 2, lines)), dma((2, lines)),
        ],
        compiler_params=pltpu.CompilerParams(
            collective_id=0, has_side_effects=True, vmem_limit_bytes=48 * 1024 * 1024
        ),
    )(value_weight[0], out_weight[0], state, gradient, keys)
    return (
        full_v.reshape(count * rows, width),
        full_o.reshape(count * rows, width),
        values.reshape(count * rows, tokens),
        d_attended.reshape(count * rows, tokens),
        window,
    )


def local(state_in, query_vectors, key_vectors, value_weight, out_weight, doc_ids, cotangent):
    rows_here = state_in.shape[0]
    blocks_here = rows_here // BLOCK
    width_here = query_vectors.shape[1]
    heads_here = width_here // HEAD_DIM
    window_rows = (REACH + 1) * rows_here
    pad_rows = REACH * rows_here
    device_index = lax.axis_index("seq")
    odd = device_index % 2 == 1
    score_scale = 1.0 / math.sqrt(HEAD_DIM)
    doc_padded = jnp.concatenate([jnp.full((REACH * blocks_here,), -1, jnp.int32), doc_ids])
    window_docs = lax.dynamic_slice_in_dim(
        doc_padded, device_index * blocks_here, (REACH + 1) * blocks_here, 0
    )
    key_docs = jnp.broadcast_to(window_docs[:, None], ((REACH + 1) * blocks_here, BLOCK)).reshape(
        -1
    )
    query_docs = key_docs[pad_rows:]
    slot_rows = jnp.arange(window_rows)
    query_rows = jnp.arange(rows_here) + pad_rows
    allowed = (key_docs[None, :] == query_docs[:, None]) & (
        slot_rows[None, :] <= query_rows[:, None]
    )
    value_rows, out_rows, raw_values, raw_gradient, window_keys = gather_rows(
        value_weight, out_weight, state_in.T, cotangent.T, key_vectors.T, odd
    )
    current = state_in.T.astype(jnp.float32)
    normed, inverse_rms = normalize(current)
    values = (raw_values * inverse_rms).astype(jnp.bfloat16)
    window_values = window_of(values, odd)
    query_heads = query_vectors.T.reshape(heads_here, HEAD_DIM, rows_here)
    key_heads = window_keys.reshape(heads_here, HEAD_DIM, window_rows)
    scores = (
        jnp.einsum("hdq,hdk->hqk", query_heads, key_heads, preferred_element_type=jnp.float32)
        * score_scale
    )
    masked = jnp.where(allowed[None], scores, -1e30)
    maxima = jnp.max(masked, axis=2, keepdims=True)
    raised = jnp.where(allowed[None], jnp.exp(masked - maxima), 0.0)
    denominator = jnp.sum(raised, axis=2, keepdims=True)
    soft_weights = (raised / denominator).astype(jnp.bfloat16)

    def attend(window_values):
        attended = jnp.einsum(
            "hqk,hdk->hdq",
            soft_weights,
            window_values.reshape(heads_here, HEAD_DIM, window_rows),
            preferred_element_type=jnp.float32,
        )
        return attended.reshape(width_here, rows_here).astype(jnp.bfloat16)

    def spread(d_attended):
        heads = d_attended.astype(jnp.bfloat16).reshape(heads_here, HEAD_DIM, rows_here)
        terms = jnp.einsum("hqk,hdq->hdk", soft_weights, heads, preferred_element_type=jnp.float32)
        terms = terms.reshape(width_here, window_rows).astype(jnp.bfloat16)
        return [
            terms[:, slot * rows_here:(slot + 1) * rows_here] for slot in range(REACH + 1)
        ]

    gradient = cotangent.T.astype(jnp.float32)
    records = []
    for unroll_step in range(UNROLL):
        terms = spread(raw_gradient)
        records.append((normed, inverse_rms))
        update = times_across(out_rows, attend(window_values))
        dvalues, update = returned_sum(terms, update.astype(jnp.bfloat16), odd)
        other_update = other_group(update)
        if unroll_step + 1 == UNROLL:
            dvalues, other_update = lax.optimization_barrier((dvalues, other_update))
        partial_grad = times_across(value_rows, dvalues).astype(jnp.bfloat16)
        current = current + head_total(update, other_update)
        d_normed = head_total(partial_grad, other_group(partial_grad))
        normed, inverse_rms = (None, None)
        if unroll_step + 1 < UNROLL:
            normed, inverse_rms = normalize(current)
        turn = UNROLL - 1 - unroll_step
        normed_turn, inverse_turn = (
            records[turn] if turn < len(records) else (normed, inverse_rms)
        )
        gradient = gradient + inverse_turn * (
            d_normed - normed_turn * jnp.mean(d_normed * normed_turn, axis=0, keepdims=True)
        )
        if unroll_step + 1 < UNROLL:
            window_values = window_of(
                times(value_rows, normed.astype(jnp.bfloat16)).astype(jnp.bfloat16), odd
            )
            raw_gradient = times(out_rows, gradient.astype(jnp.bfloat16))
    return (current.astype(jnp.bfloat16).T, gradient.T)


def solution(mesh):
    placed = (
        P("seq", None),
        P("seq", "fsdp"),
        P("seq", "fsdp"),
        P("fsdp", "seq", None),
        P("fsdp", "seq", None),
        P(),
        P("seq", None),
    )
    return jax.shard_map(
        local,
        mesh=mesh,
        in_specs=placed,
        out_specs=(P("seq", None), P("seq", None)),
        check_vma=False,
    )
```

```python
import functools
import math

import jax
import jax.numpy as jnp
from jax import lax
from jax.experimental import pallas as pl
from jax.experimental.pallas import tpu as pltpu
from jax.sharding import PartitionSpec as P

HEAD_DIM = 96
BLOCK = 128
UNROLL = 2
REACH = 4
PLANE = 4
MESH = pl.DeviceIdType.MESH


epsilon = 1e-06


def from_behind(value, axis, steps):
    count = lax.axis_size(axis)
    first, last = (max(0, -steps), min(count, count - steps))
    return lax.ppermute(value, axis, [(source, source + steps) for source in range(first, last)])


def normalize(current):
    mean_square = jnp.mean(current * current, axis=0, keepdims=True)
    inverse_rms = lax.rsqrt(mean_square + epsilon)
    return (current * inverse_rms, inverse_rms)


def other_group(own):
    if lax.axis_size("fsdp") != 2:
        wide = own.astype(jnp.float32)
        return lax.psum(wide, "fsdp") - wide
    return lax.ppermute(own, "fsdp", [(0, 1), (1, 0)])


def head_total(own, other):
    return own.astype(jnp.float32) + other.astype(jnp.float32)


def from_twin(value):
    count = lax.axis_size("seq")
    return lax.ppermute(value, "seq", [(source, source ^ 1) for source in range(count)])


def window_of(value, odd):
    first, second = from_behind(value, "seq", 2), from_behind(value, "seq", 4)
    low = from_twin(jnp.where(odd, second, first))
    high = from_twin(jnp.where(odd, first, value))
    return jnp.concatenate([second, low, first, high, value], 1)


def returned_sum(terms, update, odd):
    low, high = from_twin(terms[1]), from_twin(terms[3])
    low, high, update = lax.optimization_barrier((low, high, update))
    wide = [term.astype(jnp.float32) for term in (terms[0], terms[2], terms[4], low, high)]
    farther = wide[0] + jnp.where(odd, wide[3], 0.0)
    nearer = wide[1] + jnp.where(odd, wide[4], wide[3])
    here = wide[2] + jnp.where(odd, 0.0, wide[4])
    nearer = from_behind(nearer.astype(jnp.bfloat16), "seq", -2)
    farther = from_behind(farther.astype(jnp.bfloat16), "seq", -4)
    total = here + nearer.astype(jnp.float32) + farther.astype(jnp.float32)
    return total.astype(jnp.bfloat16), update


def times(weights, columns):
    return jnp.dot(weights, columns, preferred_element_type=jnp.float32)


def times_across(weights, columns):
    return lax.dot_general(
        weights, columns, (((0,), (0,)), ((), ())), preferred_element_type=jnp.float32
    )


def gather_kernel(
    lines, wv_ref, wo_ref, state_ref, grad_ref, keys_ref,
    full_v, full_o, slots_v, slots_o, product_v, product_o, window, raw, packed, own_sem, send_z, recv_z, send_x, recv_x, send_c, recv_c, load_sem, store_sem,
    key_send, key_recv, key_own, send_y, recv_y, factors, factor_sem,
):
    me = lax.axis_index("seq")
    group = lax.axis_index("fsdp")
    line, inner = me // PLANE, me % PLANE
    side, core = inner // 2, inner % 2
    rows, width = wv_ref.shape
    early = [0, width // 4 // 128 * 128] + [0] * (lines + 2)
    early[3] = width // 2 // 128 * 128
    shards, slots, fulls = (wv_ref, wo_ref), (slots_v, slots_o), (full_v, full_o)

    def device(other_line, other_side, other_core):
        return (other_line * PLANE + other_side * 2 + other_core, group)

    right, left = device(line + 1, side, core), device(line - 1, side, core)
    across, twin = device(line, 1 - side, core), device(line, side, 1 - core)
    has_right, has_left = line + 1 < lines, line >= 1

    diagonal = device(line + 2 * side - 1, 1 - side, core)
    has_diagonal = ((side == 1) & has_right) | ((side == 0) & has_left)
    products = (product_v, product_o)
    factor_loads = [
        pltpu.make_async_copy(ref, factors.at[w], factor_sem.at[w])
        for w, ref in enumerate((state_ref, grad_ref))
    ]
    span = keys_ref.shape[1]

    own = [pltpu.make_async_copy(shards[w], slots[w].at[me], own_sem.at[w]) for w in range(2)]
    for copy in own:
        copy.start()
    barrier = pltpu.get_barrier_semaphore()
    for there in (across, twin):
        pl.semaphore_signal(barrier, inc=1, device_id=there, device_id_type=MESH)
    for exists, there in ((has_right, right), (has_left, left), (has_diagonal, diagonal)):
        @pl.when(exists)
        def _():
            pl.semaphore_signal(barrier, inc=1, device_id=there, device_id_type=MESH)
    neighbours = 2 + sum(there.astype(jnp.int32) for there in (has_right, has_left, has_diagonal))
    pl.semaphore_wait(barrier, neighbours)
    for copy in own:
        copy.wait()

    def place(number):
        return window.at[:, number * span:(number + 1) * span]

    def key_copy(source, number, there):
        return pltpu.make_async_remote_copy(
            src_ref=source, dst_ref=place(number), send_sem=key_send.at[number],
            recv_sem=key_recv.at[number], device_id=there, device_id_type=MESH)

    count = lines * PLANE
    second = (line * PLANE + inner + 2) // PLANE
    ahead = (second * PLANE + (1 - side) * 2 + core, group)
    key_here = pltpu.make_async_copy(keys_ref, place(REACH), key_own)
    odd = core == 1

    def twin_keys(act):
        pl.when(odd & (me >= 4))(lambda: act(key_copy(place(0), 1, twin)))
        pl.when(odd & (me >= 2))(lambda: act(key_copy(place(2), 3, twin)))
        pl.when((core == 0) & (me >= 2))(lambda: act(key_copy(place(2), 1, twin)))
        pl.when(core == 0)(lambda: act(key_copy(keys_ref, 3, twin)))

    def along(w, origin, way):
        slot = slots[w].at[origin * PLANE + inner]
        return pltpu.make_async_remote_copy(
            src_ref=slot, dst_ref=slot, send_sem=send_z.at[w, way, origin],
            recv_sem=recv_z.at[w, origin], device_id=right if way == 0 else left, device_id_type=MESH)

    def along_side(w, origin, way, hops):
        slot = slots[w].at[origin * PLANE + (1 - side) * 2 + core, :, :early[hops]]
        return pltpu.make_async_remote_copy(
            src_ref=slot, dst_ref=slot, send_sem=send_y.at[w, way, origin],
            recv_sem=recv_y.at[w, origin], device_id=right if way == 0 else left, device_id_type=MESH)

    def crossing(w, origin, hops, to_me=False):
        index = origin * PLANE + ((1 - side) if to_me else side) * 2 + core
        slot = slots[w].at[index, :, early[hops]:] if early[hops] else slots[w].at[index]
        return pltpu.make_async_remote_copy(
            src_ref=slot, dst_ref=slot, send_sem=send_x.at[w, origin],
            recv_sem=recv_x.at[w, origin], device_id=across, device_id_type=MESH)

    def twinned(w, origin, far, to_me=False):
        which = (1 - side) if far else side
        slot = slots[w].at[origin * PLANE + which * 2 + ((1 - core) if to_me else core)]
        return pltpu.make_async_remote_copy(
            src_ref=slot, dst_ref=slot, send_sem=send_c.at[w, origin, far],
            recv_sem=recv_c.at[w, origin, far], device_id=twin, device_id_type=MESH)

    def arrived(w, origin, hops):
        crossing(w, origin, hops).start()
        twinned(w, origin, 0).start()

    def crossed(w, hops, origin, way):
        crossing(w, origin, hops, True).wait_recv()
        if early[hops]:
            along_side(w, origin, way, hops).wait_recv()
        if early[hops + 1]:
            if way != 1:
                pl.when(has_right)(lambda: along_side(w, origin, 0, hops + 1).start())
            if way != 0:
                pl.when(has_left)(lambda: along_side(w, origin, 1, hops + 1).start())
        twinned(w, origin, 1).start()

    def pack(w, origin, way):
        for far in range(2):
            twinned(w, origin, far, True).wait_recv()
        loads = [
            pltpu.make_async_copy(slots[w].at[origin * PLANE + k], raw.at[k], load_sem.at[k])
            for k in range(PLANE)
        ]
        for copy in loads:
            copy.start()
        for copy in loads:
            copy.wait()
        for low in range(0, width, 384):
            high = min(low + 384, width)
            for k in range(PLANE):
                packed[k * rows:(k + 1) * rows, low:high] = raw[k, :, low:high]
        store = pltpu.make_async_copy(packed, fulls[w].at[origin], store_sem)
        store.start()
        products[w][origin] = jnp.dot(
            packed[...], factors[w], preferred_element_type=jnp.float32
        )
        store.wait()

    def forward(w, step):
        for way in range(2):
            origin = line - step if way == 0 else line + step

            @pl.when((origin >= 0) if way == 0 else (origin < lines))
            def _():
                along(w, origin, way).wait_recv()

                @pl.when(has_right if way == 0 else has_left)
                def _():
                    along(w, origin, way).start()
                arrived(w, origin, step)

    def each(step, act):
        if step == 0:
            act(line, None)
            return
        pl.when(line >= step)(lambda: act(line - step, 0))
        pl.when(line + step < lines)(lambda: act(line + step, 1))

    for w in range(2):
        for exists, way in ((has_right, 0), (has_left, 1)):
            @pl.when(exists)
            def _():
                along(w, line, way).start()
        arrived(w, line, 0)
    key_here.start()
    for copy in factor_loads:
        copy.start()
    for copy in factor_loads:
        copy.wait()
    pl.when(me + 2 < count)(lambda: key_copy(keys_ref, 2, ahead).start())
    pl.when(has_right)(lambda: key_copy(keys_ref, 0, right).start())
    order = [(step, w) for step in range(lines) for w in range(2)]
    turns = len(order)
    for turn in range(2, turns + 3):
        if turn < turns:
            forward(order[turn][1], order[turn][0])
        if 0 <= turn - 3 < turns:
            step, w = order[turn - 3]
            each(step, functools.partial(pack, w))
        if 0 <= turn - 2 < turns:
            step, w = order[turn - 2]
            each(step, functools.partial(crossed, w, step))
        if turn == 5:
            pl.when(me >= 2)(lambda: key_copy(keys_ref, 2, ahead).wait_recv())
            pl.when(me >= 4)(lambda: key_copy(keys_ref, 0, right).wait_recv())
            twin_keys(lambda copy: copy.start())
    pl.when(me >= 3)(lambda: key_copy(keys_ref, 1, twin).wait_recv())
    pl.when(me >= 1)(lambda: key_copy(keys_ref, 3, twin).wait_recv())
    twin_keys(lambda copy: copy.wait_send())
    pl.when(me + 2 < count)(lambda: key_copy(keys_ref, 2, ahead).wait_send())
    pl.when(has_right)(lambda: key_copy(keys_ref, 0, right).wait_send())
    key_here.wait()
    for w in range(2):
        for step in range(lines):
            each(step, lambda origin, way: crossing(w, origin, step).wait_send())
            pl.when(has_right & (line >= step))(lambda: along(w, line - step, 0).wait_send())
            pl.when(has_left & (line + step < lines))(lambda: along(w, line + step, 1).wait_send())
            if early[step + 1]:
                pl.when(has_right & (line >= step))(
                    lambda: along_side(w, line - step, 0, step + 1).wait_send()
                )
                pl.when(has_left & (line + step < lines))(
                    lambda: along_side(w, line + step, 1, step + 1).wait_send()
                )
        for origin in range(lines):
            for far in range(2):
                twinned(w, origin, far).wait_send()


def gather_rows(value_weight, out_weight, state, gradient, keys, odd):
    count = lax.axis_size("seq")
    rows, width = value_weight.shape[1:]
    tokens, channels = state.shape[1], keys.shape[0]
    lines = count // PLANE
    if count % PLANE or (PLANE * rows) % 16 or rows % 2:
        value_rows, out_rows = (
            lax.all_gather(weight, "seq", axis=1, tiled=True)[0]
            for weight in (value_weight, out_weight)
        )
        window = window_of(keys, odd)
        return value_rows, out_rows, times(value_rows, state), times(out_rows, gradient), window
    full = jax.ShapeDtypeStruct((lines, PLANE * rows, width), jnp.bfloat16)
    slot = jax.ShapeDtypeStruct((count, rows, width), jnp.bfloat16)
    product = jax.ShapeDtypeStruct((lines, PLANE * rows, tokens), jnp.float32)
    window = jax.ShapeDtypeStruct((channels, (REACH + 1) * tokens), jnp.bfloat16)
    dma = pltpu.SemaphoreType.DMA
    anywhere, vector = (pl.BlockSpec(memory_space=space) for space in (pl.ANY, pltpu.VMEM))
    full_v, full_o, _, _, values, d_attended, window = pl.pallas_call(
        functools.partial(gather_kernel, lines),
        out_shape=(full, full, slot, slot, product, product, window),
        in_specs=[anywhere] * 5,
        out_specs=[anywhere] * 4 + [vector, vector, anywhere],
        scratch_shapes=[
            pltpu.VMEM((PLANE, rows, width), jnp.bfloat16),
            pltpu.VMEM((PLANE * rows, width), jnp.bfloat16),
            dma((2,)),
            dma((2, 2, lines)), dma((2, lines)),
            dma((2, lines)), dma((2, lines)),
            dma((2, lines, 2)), dma((2, lines, 2)),
            dma((PLANE,)), dma,
            dma((REACH,)), dma((REACH,)), dma,
            dma((2, 2, lines)), dma((2, lines)),
            pltpu.VMEM((2, width, tokens), jnp.bfloat16), dma((2,)),
        ],
        compiler_params=pltpu.CompilerParams(
            collective_id=0, has_side_effects=True, vmem_limit_bytes=58 * 1024 * 1024
        ),
    )(value_weight[0], out_weight[0], state, gradient, keys)
    return (
        full_v.reshape(count * rows, width),
        full_o.reshape(count * rows, width),
        values.reshape(count * rows, tokens),
        d_attended.reshape(count * rows, tokens),
        window,
    )


def local(state_in, query_vectors, key_vectors, value_weight, out_weight, doc_ids, cotangent):
    rows_here = state_in.shape[0]
    blocks_here = rows_here // BLOCK
    width_here = query_vectors.shape[1]
    heads_here = width_here // HEAD_DIM
    window_rows = (REACH + 1) * rows_here
    pad_rows = REACH * rows_here
    device_index = lax.axis_index("seq")
    odd = device_index % 2 == 1
    score_scale = 1.0 / math.sqrt(HEAD_DIM)
    doc_padded = jnp.concatenate([jnp.full((REACH * blocks_here,), -1, jnp.int32), doc_ids])
    window_docs = lax.dynamic_slice_in_dim(
        doc_padded, device_index * blocks_here, (REACH + 1) * blocks_here, 0
    )
    key_docs = jnp.broadcast_to(window_docs[:, None], ((REACH + 1) * blocks_here, BLOCK)).reshape(
        -1
    )
    query_docs = key_docs[pad_rows:]
    slot_rows = jnp.arange(window_rows)
    query_rows = jnp.arange(rows_here) + pad_rows
    allowed = (key_docs[None, :] == query_docs[:, None]) & (
        slot_rows[None, :] <= query_rows[:, None]
    )
    value_rows, out_rows, raw_values, raw_gradient, window_keys = gather_rows(
        value_weight, out_weight, state_in.T, cotangent.T, key_vectors.T, odd
    )
    current = state_in.T.astype(jnp.float32)
    normed, inverse_rms = normalize(current)
    values = (raw_values * inverse_rms).astype(jnp.bfloat16)
    window_values = window_of(values, odd)
    query_heads = query_vectors.T.reshape(heads_here, HEAD_DIM, rows_here)
    key_heads = window_keys.reshape(heads_here, HEAD_DIM, window_rows)
    scores = (
        jnp.einsum("hdq,hdk->hqk", query_heads, key_heads, preferred_element_type=jnp.float32)
        * score_scale
    )
    masked = jnp.where(allowed[None], scores, -1e30)
    maxima = jnp.max(masked, axis=2, keepdims=True)
    raised = jnp.where(allowed[None], jnp.exp(masked - maxima), 0.0)
    denominator = jnp.sum(raised, axis=2, keepdims=True)
    soft_weights = (raised / denominator).astype(jnp.bfloat16)

    def attend(window_values):
        attended = jnp.einsum(
            "hqk,hdk->hdq",
            soft_weights,
            window_values.reshape(heads_here, HEAD_DIM, window_rows),
            preferred_element_type=jnp.float32,
        )
        return attended.reshape(width_here, rows_here).astype(jnp.bfloat16)

    def spread(d_attended):
        heads = d_attended.astype(jnp.bfloat16).reshape(heads_here, HEAD_DIM, rows_here)
        terms = jnp.einsum("hqk,hdq->hdk", soft_weights, heads, preferred_element_type=jnp.float32)
        terms = terms.reshape(width_here, window_rows).astype(jnp.bfloat16)
        return [
            terms[:, slot * rows_here:(slot + 1) * rows_here] for slot in range(REACH + 1)
        ]

    gradient = cotangent.T.astype(jnp.float32)
    records = []
    for unroll_step in range(UNROLL):
        terms = spread(raw_gradient)
        records.append((normed, inverse_rms))
        update = times_across(out_rows, attend(window_values))
        dvalues, update = returned_sum(terms, update.astype(jnp.bfloat16), odd)
        other_update = other_group(update)
        if unroll_step + 1 == UNROLL:
            dvalues, other_update = lax.optimization_barrier((dvalues, other_update))
        partial_grad = times_across(value_rows, dvalues).astype(jnp.bfloat16)
        current = current + head_total(update, other_update)
        d_normed = head_total(partial_grad, other_group(partial_grad))
        normed, inverse_rms = (None, None)
        if unroll_step + 1 < UNROLL:
            normed, inverse_rms = normalize(current)
        turn = UNROLL - 1 - unroll_step
        normed_turn, inverse_turn = (
            records[turn] if turn < len(records) else (normed, inverse_rms)
        )
        gradient = gradient + inverse_turn * (
            d_normed - normed_turn * jnp.mean(d_normed * normed_turn, axis=0, keepdims=True)
        )
        if unroll_step + 1 < UNROLL:
            window_values = window_of(
                times(value_rows, normed.astype(jnp.bfloat16)).astype(jnp.bfloat16), odd
            )
            raw_gradient = times(out_rows, gradient.astype(jnp.bfloat16))
    return (current.astype(jnp.bfloat16).T, gradient.T)


def solution(mesh):
    placed = (
        P("seq", None),
        P("seq", "fsdp"),
        P("seq", "fsdp"),
        P("fsdp", "seq", None),
        P("fsdp", "seq", None),
        P(),
        P("seq", None),
    )
    return jax.shard_map(
        local,
        mesh=mesh,
        in_specs=placed,
        out_specs=(P("seq", None), P("seq", None)),
        check_vma=False,
    )
```
